32 devices in a mesh: gx: 8 (over z, y), gy: 4 (over x, core).
Axes of the slice: x: 2, y: 2, z: 4, core: 2. Of those that a mesh axis runs over, the one named last changes fastest.
Arguments:
- adjoint_state: float32 [5, 16, 128, 512], P(None, None, 'gx', 'gy'), may hold values from -6 to 6
- trajectory: float32 [2, 5, 16, 128, 512], P(None, None, None, 'gx', 'gy'), may hold values from -3 to 3
- ray_resid: float32 [16384, 2, 128], P(('gx', 'gy')), may hold values from -6 to 6
- ray_angle: float32 [16384, 128], P(('gx', 'gy')), may hold values from -3.140625 to 3.140625
- ray_slope: float32 [16384, 128], P(('gx', 'gy')), may hold values from 0.5 to 4
- ray_dest: int32 [16384, 1], P(('gx', 'gy')), may hold values from 0 to 31; in each aligned block of 512 rows (0 to 511, 512 to 1023, ...) at most 32 rows name the same one
- gate_cell: int32 [16384, 128], P(('gx', 'gy')), may hold values from 0 to 32767
Outputs:
- initial_grad: float32 [5, 16, 128, 512], P(None, None, 'gx', 'gy')
The draws below stay inside these ranges and needn't reach their ends.
Inputs may be any that keep to these rules, and one draw needn't show every extreme that they name: `ray_dest`: each aligned block of 512 ray groups (the ray groups of one device) names any one tile at most 32 times; some tile is named exactly 32 times.
All inputs are finite; a program needn't handle non-finite values.
Results may differ from the reference program's by a relative error of at most 0.00002.
Values sent between devices are 32-bit elements; how exact they have to be, the bound alone decides.
A program may use at most 192 MiB of HBM per device.

```python
import math
import jax
import jax.numpy as jnp
import numpy as np

CX = 16
CY = 128
NZ = 16
RG = 512
GATES = 128
FIELDS = 5
STEPS = 2
NX = 128
NY = 512
RAYS = 16384
CAP = 32
N_GY = 4
DEVICES = 32


def with_ends(drawn, stream_key, smallest, top_value):
    extent = drawn.shape
    place = [jax.random.randint(jax.random.fold_in(stream_key, axis), (), 0, extent[axis]) for axis in range(len(extent))]
    drawn = drawn.at[tuple(place)].set(smallest)
    longest = extent.index(max(extent))
    place[longest] = (place[longest] + 1) % extent[longest]
    return drawn.at[tuple(place)].set(top_value)


def block_levels(own_key, dims, split, low, top_value):
    def one(axis_at, parts):
        heights = jax.random.uniform(jax.random.fold_in(jax.random.fold_in(own_key, 6), axis_at), (parts,), jnp.float32, low / len(split), top_value / len(split))
        return jnp.repeat(jnp.exp(heights), dims[axis_at] // parts).reshape((-1,) + (1,) * (len(dims) - axis_at - 1))

    level = one(*split[0])
    for cut in split[1:]:
        level = level * one(*cut)
    return level


def shared_out(stream_key, own, number, rows, amount, top, limit, skew):
    order = jax.random.permutation(stream_key, amount)
    crowded, ordinary = shares(amount, rows * top, limit, skew, True), shares(amount, rows * top, limit, skew, False)
    places = jnp.arange(amount)

    def named(tallies, offset_by):
        used = int((tallies > 0).sum())
        fixed = max(1, used // 4)
        moved = fixed + (places - fixed + offset_by * (used - fixed)) % max(1, amount - fixed)
        return jnp.zeros((amount,), jnp.int32).at[order[jnp.where(places < fixed, places, moved)]].set(jnp.asarray(tallies, jnp.int32))

    tallies = jnp.where(number % 4 == 0, named(crowded, number // 4), named(ordinary, number - number // 4 - 1))
    mixed = jax.random.permutation(jax.random.fold_in(own, 3), amount)
    source_of, taker = mixed[0:amount // 2 * 2:2], mixed[1:amount // 2 * 2:2]
    margin = jnp.minimum(tallies[source_of] - 1, limit - tallies[taker]) // 2
    margin = jnp.where((source_of == order[0]) | (taker == order[0]) | (tallies[taker] == 0), 0, jnp.maximum(margin, 0))
    moved = jax.random.randint(jax.random.fold_in(own, 4), (amount // 2,), 0, 1 << 20) % (margin + 1)
    tallies = tallies.at[source_of].add(-moved).at[taker].add(moved)
    items = jnp.searchsorted(jnp.cumsum(tallies), jnp.arange(rows * top), side="right").astype(jnp.int32)
    listing = items.reshape(top, rows).T
    listing = listing[jax.random.permutation(jax.random.fold_in(own, 1), rows)]
    offset_by = jax.random.randint(jax.random.fold_in(own, 2), (rows, 1), 0, top)
    return jnp.take_along_axis(listing, (jnp.arange(top)[None, :] + offset_by) % top, axis=1)


def shares(count, total, bound, skew, full):
    loads = [(1 << 20) // math.isqrt(standing ** skew) + 1 for standing in range(1, count + 1)]
    largest = bound if full else min(bound, max(-(-total // count), total * loads[0] // sum(loads)))
    least = 1 if total - largest >= count - 1 else 0
    holding, rest = [largest] + [least] * (count - 1), total - largest - least * (count - 1)
    while rest > 0:
        candidates = [i for i in range(1, count) if holding[i] < largest] or [i for i in range(1, count) if holding[i] < bound]
        pool, budget = sum([loads[i] for i in candidates]), rest
        for i in candidates:
            addition = min(bound - holding[i], max(1, budget * loads[i] // pool), rest)
            holding[i] = holding[i] + addition
            rest = rest - addition
    return np.array(holding)


def centred(key, dims, spread, most, cuts=(), held_as=jnp.bfloat16):
    drawn = jax.random.normal(key, dims, jnp.float32) * spread
    if len(cuts) > 0:
        drawn = block_levels(key, dims, cuts, -0.22, 0.18) * drawn
    return jnp.clip(drawn, min=-most, max=most).astype(held_as)


def setup_inputs(seed: int = 0) -> dict:
    key_list = jax.random.split(jax.random.key(seed), 8)
    adjoint_state = centred(key_list[0], (FIELDS, NZ, NX, NY), 1.0, 6.0, ((2, 8), (3, 4)), jnp.float32)
    trajectory = centred(key_list[1], (STEPS, FIELDS, NZ, NX, NY), 0.5, 3.0, ((3, 8), (4, 4)), jnp.float32)
    ray_resid = centred(key_list[2], (RAYS, 2, GATES), 1.0, 6.0, ((0, 32),), jnp.float32)
    ray_angle = jnp.clip(jax.random.uniform(key_list[3], (RAYS, GATES), jnp.float32, -3.140625, 3.140625), -3.140625, 3.140625)
    ray_slope = jnp.clip(jnp.exp(math.log(4.0) - 2.0794415 * jax.random.uniform(key_list[4], (RAYS, GATES), jnp.float32) ** block_levels(key_list[4], (RAYS, GATES), ((0, 32),), -0.2, 0.2)), 0.5, 4.0)
    ray_dest_keys = jax.random.split(jax.random.fold_in(key_list[5], 1), RAYS // RG)
    ray_dest_turns = jax.random.permutation(jax.random.fold_in(key_list[5], 3), RAYS // RG)
    ray_dest = jax.vmap(lambda own, number: shared_out(jax.random.fold_in(key_list[5], 2), own, number, RG, DEVICES, 1, CAP, 2))(ray_dest_keys, ray_dest_turns).reshape((RAYS, 1))
    gate_cell = with_ends(jax.random.randint(key_list[6], (RAYS, GATES), 0, NZ * CX * CY), jax.random.fold_in(key_list[6], 1), 0, (NZ * CX * CY) - 1).astype(jnp.int32)
    return dict(adjoint_state=adjoint_state, trajectory=trajectory, ray_resid=ray_resid, ray_angle=ray_angle, ray_slope=ray_slope, ray_dest=ray_dest, gate_cell=gate_cell)


diffusion = 0.1
latent = 2.0

def f_valid(state_pad, traj_pad):
    center = state_pad[..., 1:-1, 1:-1]
    diff_x = 0.5 * (state_pad[..., 2:, 1:-1] - state_pad[..., :-2, 1:-1])
    diff_y = 0.5 * (state_pad[..., 1:-1, 2:] - state_pad[..., 1:-1, :-2])
    laplace = state_pad[..., 2:, 1:-1] + state_pad[..., :-2, 1:-1] + state_pad[..., 1:-1, 2:] + state_pad[..., 1:-1, :-2] - 4.0 * center
    grad_x = 0.5 * (traj_pad[..., 2:, 1:-1] - traj_pad[..., :-2, 1:-1])
    grad_y = 0.5 * (traj_pad[..., 1:-1, 2:] - traj_pad[..., 1:-1, :-2])
    wind_u = traj_pad[0, :, 1:-1, 1:-1]
    wind_v = traj_pad[1, :, 1:-1, 1:-1]
    advected = center - (wind_u * diff_x + wind_v * diff_y) - (center[0] * grad_x + center[1] * grad_y) + diffusion * laplace
    convert = 0.3 * jax.nn.sigmoid(traj_pad[2, :, 1:-1, 1:-1])
    falling = 0.3 * jax.nn.sigmoid(traj_pad[4, :, 1:-1, 1:-1])
    condensed = convert * advected[3]
    rain_old = advected[4]
    from_above = jnp.concatenate([rain_old[1:], jnp.zeros_like(rain_old[:1])], axis=0)
    rain_new = rain_old + condensed + falling * (from_above - rain_old)
    return jnp.stack([advected[0], advected[1], advected[2] + latent * condensed, advected[3] - condensed, rain_new])

def pad_grid(field):
    return jnp.pad(field, ((0, 0), (0, 0), (1, 1), (1, 1)))

def tangent_step(pert, traj_now):
    return f_valid(pad_grid(pert), pad_grid(traj_now))

def reference(adjoint_state, trajectory, ray_resid, ray_angle, ray_slope, ray_dest, gate_cell):
    velocity = ray_resid[:, 0]
    contrib = jnp.stack([jnp.sin(ray_angle) * velocity, jnp.cos(ray_angle) * velocity, ray_slope * ray_resid[:, 1]], axis=1)
    target = ray_dest[:, 0]
    level_of = gate_cell // (CX * CY)
    remain = gate_cell % (CX * CY)
    row_in = remain // CY
    col_in = remain % CY
    glob_x = (target // N_GY)[:, None] * CX + row_in
    glob_y = (target % N_GY)[:, None] * CY + col_in
    flat_index = (level_of * (NX * NY) + glob_x * NY + glob_y).reshape(-1).astype(jnp.int32)
    values = jnp.transpose(contrib, (1, 0, 2)).reshape(3, -1)
    forcing = jnp.zeros((3, NZ * NX * NY), jnp.float32).at[:, flat_index].add(values)
    forcing = forcing.reshape(3, NZ, NX, NY)
    blank_field = jnp.zeros_like(forcing[0])
    result = adjoint_state + jnp.stack([forcing[0], forcing[1], blank_field, blank_field, forcing[2]])
    for section in (1, 0):
        traj_now = trajectory[section]
        primal = jnp.zeros_like(result)
        unused, pullback = jax.vjp(lambda pert: tangent_step(pert, traj_now), primal)
        result = pullback(result)[0]
    return result
```

```python
import jax
import jax.numpy as jnp
from jax import lax
from jax.experimental import pallas as pl
from jax.experimental.pallas import tpu as pltpu
from jax.sharding import PartitionSpec as P

diffusion = 0.1
latent = 2.0


def with_halo(block, sides, width):
    for axis, dim in sides:
        count = lax.axis_size(axis)
        forward = [(i, i + 1) for i in range(count - 1)]
        backward = [(target, source) for source, target in forward]
        low = lax.ppermute(
            lax.slice_in_dim(block, block.shape[dim] - width, None, axis=dim), axis, forward
        )
        high = lax.ppermute(lax.slice_in_dim(block, 0, width, axis=dim), axis, backward)
        block = jnp.concatenate([low, block, high], axis=dim)
    return block


def f_valid(state_pad, traj_pad):
    center = state_pad[..., 1:-1, 1:-1]
    diff_x = 0.5 * (state_pad[..., 2:, 1:-1] - state_pad[..., :-2, 1:-1])
    diff_y = 0.5 * (state_pad[..., 1:-1, 2:] - state_pad[..., 1:-1, :-2])
    laplace = (
        state_pad[..., 2:, 1:-1]
        + state_pad[..., :-2, 1:-1]
        + state_pad[..., 1:-1, 2:]
        + state_pad[..., 1:-1, :-2]
        - 4.0 * center
    )
    grad_x = 0.5 * (traj_pad[..., 2:, 1:-1] - traj_pad[..., :-2, 1:-1])
    grad_y = 0.5 * (traj_pad[..., 1:-1, 2:] - traj_pad[..., 1:-1, :-2])
    wind_u = traj_pad[0, :, 1:-1, 1:-1]
    wind_v = traj_pad[1, :, 1:-1, 1:-1]
    advected = (
        center
        - (wind_u * diff_x + wind_v * diff_y)
        - (center[0] * grad_x + center[1] * grad_y)
        + diffusion * laplace
    )
    convert = 0.3 * jax.nn.sigmoid(traj_pad[2, :, 1:-1, 1:-1])
    falling = 0.3 * jax.nn.sigmoid(traj_pad[4, :, 1:-1, 1:-1])
    condensed = convert * advected[3]
    rain_old = advected[4]
    from_above = jnp.concatenate([rain_old[1:], jnp.zeros_like(rain_old[:1])], axis=0)
    rain_new = rain_old + condensed + falling * (from_above - rain_old)
    return jnp.stack(
        [
            advected[0],
            advected[1],
            advected[2] + latent * condensed,
            advected[3] - condensed,
            rain_new,
        ]
    )


def adjoint_region(cot_ext, traj_ext):
    primal = jnp.zeros_like(traj_ext)
    unused, pullback = jax.vjp(lambda state_pad: f_valid(state_pad, traj_ext), primal)
    cotangent = pullback(cot_ext)[0]
    return cotangent[..., 2:-2, 2:-2]


def scatter_kernel(got, out, acc, lhs, rhs):
    sources, slots, channels, gates = got.shape
    rows, cols = out.shape[1:]
    bf16 = jnp.bfloat16
    acc[...] = jnp.zeros_like(acc)
    iota_col = lax.broadcasted_iota(jnp.int32, (cols, gates), 0).astype(jnp.float32).astype(bf16)
    iota_row = lax.broadcasted_iota(jnp.int32, (rows, gates), 0).astype(jnp.float32).astype(bf16)
    zero_col = jnp.zeros((cols, gates), bf16)
    zero_row = jnp.zeros((rows, gates), bf16)
    one_row = jnp.ones((rows, gates), bf16)

    def one_source(source, carry):
        for slot in range(slots):
            span = slice(slot * gates, (slot + 1) * gates)
            cell = got[source, slot, pl.ds(3, 1), :].astype(jnp.int32)
            row = (cell // cols).astype(jnp.float32)
            col = (cell % cols).astype(jnp.float32)
            row = jnp.broadcast_to(row, (rows, gates)).astype(bf16)
            col = jnp.broadcast_to(col, (cols, gates)).astype(bf16)
            hit = iota_col == col
            for channel in range(3):
                value = got[source, slot, pl.ds(channel, 1), :]
                high = value.astype(bf16).astype(jnp.float32)
                for part, piece in enumerate((high, value - high)):
                    piece = jnp.broadcast_to(piece, (cols, gates)).astype(bf16)
                    at = (2 * channel + part) * cols
                    lhs[at : at + cols, span] = jnp.where(hit, piece, zero_col)
            rhs[:, span] = jnp.where(iota_row == row, one_row, zero_row)
        acc[...] += lax.dot_general(
            lhs[...], rhs[...], (((1,), (1,)), ((), ())), preferred_element_type=jnp.float32
        )
        return carry

    lax.fori_loop(0, sources, one_source, 0)
    for channel in range(3):
        at = 2 * channel * cols
        out[channel] = (acc[at : at + cols, :] + acc[at + cols : at + 2 * cols, :]).T


def scatter(got, rows, cols):
    sources, slots, channels, gates = got.shape
    return pl.pallas_call(
        scatter_kernel,
        out_shape=jax.ShapeDtypeStruct((3, rows, cols), jnp.float32),
        in_specs=[pl.BlockSpec(memory_space=pltpu.VMEM)],
        out_specs=pl.BlockSpec(memory_space=pltpu.VMEM),
        scratch_shapes=[
            pltpu.VMEM((6 * cols, rows), jnp.float32),
            pltpu.VMEM((6 * cols, slots * gates), jnp.bfloat16),
            pltpu.VMEM((rows, slots * gates), jnp.bfloat16),
        ],
        compiler_params=pltpu.CompilerParams(vmem_limit_bytes=40 * 2**20),
        name="scatter",
    )(got)


def pack_kernel(from_ray, packed, out):
    rays = packed.shape[0]

    def one_slot(slot, carry):
        ray = from_ray[slot]
        block = packed[jnp.minimum(ray, rays - 1)]
        out[slot] = jnp.where(ray < rays, block, jnp.zeros_like(block))
        return carry

    lax.fori_loop(0, out.shape[0], one_slot, 0, unroll=8)


def pack(from_ray, packed):
    return pl.pallas_call(
        pack_kernel,
        out_shape=jax.ShapeDtypeStruct(from_ray.shape + packed.shape[1:], jnp.float32),
        in_specs=[pl.BlockSpec(memory_space=pltpu.SMEM), pl.BlockSpec(memory_space=pltpu.VMEM)],
        out_specs=pl.BlockSpec(memory_space=pltpu.VMEM),
        compiler_params=pltpu.CompilerParams(vmem_limit_bytes=16 * 2**20),
        name="pack",
    )(from_ray, packed)


def local(adjoint_state, trajectory, ray_resid, ray_angle, ray_slope, ray_dest, gate_cell):
    tiles_x = lax.axis_size("gx")
    tiles_y = lax.axis_size("gy")
    devices = tiles_x * tiles_y
    ray_count = ray_resid.shape[0]
    gate_count = ray_resid.shape[2]
    capacity = max(2, 2 * ray_count // devices)
    velocity = ray_resid[:, 0]
    contrib = jnp.stack(
        [jnp.sin(ray_angle) * velocity, jnp.cos(ray_angle) * velocity, ray_slope * ray_resid[:, 1]],
        axis=1,
    )
    target = ray_dest[:, 0]
    positions = jnp.arange(ray_count, dtype=jnp.int32)
    earlier = (target[:, None] == target[None, :]) & (positions[None, :] < positions[:, None])
    slot_rank = jnp.sum(earlier.astype(jnp.int32), axis=1)
    slot_index = target * capacity + slot_rank
    slots_total = devices * capacity
    slot_ids = jnp.arange(slots_total, dtype=jnp.int32)
    matches = slot_index[None, :] == slot_ids[:, None]
    filled = jnp.any(matches, axis=1)
    source = jnp.sum(jnp.where(matches, positions[None, :], 0), axis=1)
    packed = jnp.concatenate([contrib, gate_cell[:, None].astype(jnp.float32)], axis=1)
    values = pack(jnp.where(filled, source, ray_count), packed)
    values = values.reshape(devices, capacity, 4, gate_count)
    got = lax.all_to_all(values, ("gx", "gy"), split_axis=0, concat_axis=0, tiled=True)
    levels = adjoint_state.shape[1]
    cols_x = adjoint_state.shape[2]
    cols_y = adjoint_state.shape[3]
    forcing = scatter(got, levels * cols_x, cols_y)
    forcing = forcing.reshape(3, levels, cols_x, cols_y)
    blank_field = jnp.zeros_like(forcing[0])
    result = adjoint_state + jnp.stack(
        [forcing[0], forcing[1], blank_field, blank_field, forcing[2]]
    )
    rim_width = 2
    traj_ext = with_halo(trajectory, (("gx", 3), ("gy", 4)), rim_width)
    for section in (1, 0):
        extended = with_halo(result, (("gx", 2), ("gy", 3)), 1)
        result = adjoint_region(extended, traj_ext[section])
    return result


def solution(mesh):
    return jax.shard_map(
        local,
        mesh=mesh,
        in_specs=(
            P(None, None, "gx", "gy"),
            P(None, None, None, "gx", "gy"),
            P(("gx", "gy"), None, None),
            P(("gx", "gy"), None),
            P(("gx", "gy"), None),
            P(("gx", "gy"), None),
            P(("gx", "gy"), None),
        ),
        out_specs=P(None, None, "gx", "gy"),
        check_vma=False,
    )
```

```python
import jax
import jax.numpy as jnp
from jax import lax
from jax.experimental import pallas as pl
from jax.experimental.pallas import tpu as pltpu
from jax.sharding import PartitionSpec as P

diffusion = 0.1
latent = 2.0


def from_next(edge, axis):
    count = lax.axis_size(axis)
    return lax.ppermute(edge, axis, [(i + 1, i) for i in range(count - 1)])


def from_previous(edge, axis):
    count = lax.axis_size(axis)
    return lax.ppermute(edge, axis, [(i, i + 1) for i in range(count - 1)])


def shifted(above, below, axis, dim):
    size = above.shape[dim]
    last = from_next(lax.slice_in_dim(above, 0, 1, axis=dim), axis)
    first = from_previous(lax.slice_in_dim(below, size - 1, size, axis=dim), axis)
    up = jnp.concatenate([lax.slice_in_dim(above, 1, size, axis=dim), last], axis=dim)
    down = jnp.concatenate([first, lax.slice_in_dim(below, 0, size - 1, axis=dim)], axis=dim)
    return up, down


def adjoint_step(cot, traj, slope_x, slope_y):
    convert = 0.3 * jax.nn.sigmoid(traj[2])
    falling = 0.3 * jax.nn.sigmoid(traj[4])
    condensed = convert * (latent * cot[2] - cot[3] + cot[4])
    fallen = falling * cot[4]
    into_below = jnp.concatenate([jnp.zeros_like(fallen[:1]), fallen[:-1]], axis=0)
    own = jnp.stack([cot[0], cot[1], cot[2], cot[3] + condensed, cot[4] - fallen + into_below])
    half_u, half_v = 0.5 * traj[0], 0.5 * traj[1]
    up_x, down_x = shifted((diffusion + half_u) * own, (diffusion - half_u) * own, "gx", 2)
    up_y, down_y = shifted((diffusion + half_v) * own, (diffusion - half_v) * own, "gy", 3)
    result = (1.0 - 4.0 * diffusion) * own + up_x + down_x + up_y + down_y
    blank = jnp.zeros_like(traj[0])
    wind = jnp.stack(
        [jnp.sum(own * slope_x, axis=0), jnp.sum(own * slope_y, axis=0), blank, blank, blank]
    )
    return result - wind


def scatter_kernel(got, out, acc, lhs, rhs):
    sources, slots, channels, gates = got.shape
    rows, cols = out.shape[1:]
    bf16 = jnp.bfloat16
    acc[...] = jnp.zeros_like(acc)
    iota_col = lax.broadcasted_iota(jnp.int32, (cols, gates), 0).astype(jnp.float32).astype(bf16)
    iota_row = lax.broadcasted_iota(jnp.int32, (rows, gates), 0).astype(jnp.float32).astype(bf16)
    zero_col = jnp.zeros((cols, gates), bf16)
    zero_row = jnp.zeros((rows, gates), bf16)
    one_row = jnp.ones((rows, gates), bf16)

    def one_source(source, carry):
        for slot in range(slots):
            span = slice(slot * gates, (slot + 1) * gates)
            cell = got[source, slot, pl.ds(3, 1), :].astype(jnp.int32)
            row = (cell // cols).astype(jnp.float32)
            col = (cell % cols).astype(jnp.float32)
            row = jnp.broadcast_to(row, (rows, gates)).astype(bf16)
            col = jnp.broadcast_to(col, (cols, gates)).astype(bf16)
            hit = iota_col == col
            for channel in range(3):
                value = got[source, slot, pl.ds(channel, 1), :]
                high = value.astype(bf16).astype(jnp.float32)
                for part, piece in enumerate((high, value - high)):
                    piece = jnp.broadcast_to(piece, (cols, gates)).astype(bf16)
                    at = (2 * channel + part) * cols
                    lhs[at : at + cols, span] = jnp.where(hit, piece, zero_col)
            rhs[:, span] = jnp.where(iota_row == row, one_row, zero_row)
        acc[...] += lax.dot_general(
            lhs[...], rhs[...], (((1,), (1,)), ((), ())), preferred_element_type=jnp.float32
        )
        return carry

    lax.fori_loop(0, sources, one_source, 0)
    for channel in range(3):
        at = 2 * channel * cols
        out[channel] = (acc[at : at + cols, :] + acc[at + cols : at + 2 * cols, :]).T


def scatter(got, rows, cols):
    sources, slots, channels, gates = got.shape
    return pl.pallas_call(
        scatter_kernel,
        out_shape=jax.ShapeDtypeStruct((3, rows, cols), jnp.float32),
        in_specs=[pl.BlockSpec(memory_space=pltpu.VMEM)],
        out_specs=pl.BlockSpec(memory_space=pltpu.VMEM),
        scratch_shapes=[
            pltpu.VMEM((6 * cols, rows), jnp.float32),
            pltpu.VMEM((6 * cols, slots * gates), jnp.bfloat16),
            pltpu.VMEM((rows, slots * gates), jnp.bfloat16),
        ],
        compiler_params=pltpu.CompilerParams(vmem_limit_bytes=40 * 2**20),
        name="scatter",
    )(got)


def pack_kernel(from_ray, packed, out):
    rays = packed.shape[0]

    def one_slot(slot, carry):
        ray = from_ray[slot]
        block = packed[jnp.minimum(ray, rays - 1)]
        out[slot] = jnp.where(ray < rays, block, jnp.zeros_like(block))
        return carry

    lax.fori_loop(0, out.shape[0], one_slot, 0, unroll=8)


def pack(from_ray, packed):
    return pl.pallas_call(
        pack_kernel,
        out_shape=jax.ShapeDtypeStruct(from_ray.shape + packed.shape[1:], jnp.float32),
        in_specs=[pl.BlockSpec(memory_space=pltpu.SMEM), pl.BlockSpec(memory_space=pltpu.VMEM)],
        out_specs=pl.BlockSpec(memory_space=pltpu.VMEM),
        compiler_params=pltpu.CompilerParams(vmem_limit_bytes=16 * 2**20),
        name="pack",
    )(from_ray, packed)


def local(adjoint_state, trajectory, ray_resid, ray_angle, ray_slope, ray_dest, gate_cell):
    tiles_x = lax.axis_size("gx")
    tiles_y = lax.axis_size("gy")
    devices = tiles_x * tiles_y
    ray_count = ray_resid.shape[0]
    gate_count = ray_resid.shape[2]
    capacity = max(2, 2 * ray_count // devices)
    velocity = ray_resid[:, 0]
    contrib = jnp.stack(
        [jnp.sin(ray_angle) * velocity, jnp.cos(ray_angle) * velocity, ray_slope * ray_resid[:, 1]],
        axis=1,
    )
    target = ray_dest[:, 0]
    positions = jnp.arange(ray_count, dtype=jnp.int32)
    earlier = (target[:, None] == target[None, :]) & (positions[None, :] < positions[:, None])
    slot_rank = jnp.sum(earlier.astype(jnp.int32), axis=1)
    slot_index = target * capacity + slot_rank
    slots_total = devices * capacity
    slot_ids = jnp.arange(slots_total, dtype=jnp.int32)
    matches = slot_index[None, :] == slot_ids[:, None]
    filled = jnp.any(matches, axis=1)
    source = jnp.sum(jnp.where(matches, positions[None, :], 0), axis=1)
    packed = jnp.concatenate([contrib, gate_cell[:, None].astype(jnp.float32)], axis=1)
    values = pack(jnp.where(filled, source, ray_count), packed)
    values = values.reshape(devices, capacity, 4, gate_count)
    got = lax.all_to_all(values, ("gx", "gy"), split_axis=0, concat_axis=0, tiled=True)
    levels = adjoint_state.shape[1]
    cols_x = adjoint_state.shape[2]
    cols_y = adjoint_state.shape[3]
    forcing = scatter(got, levels * cols_x, cols_y)
    forcing = forcing.reshape(3, levels, cols_x, cols_y)
    blank_field = jnp.zeros_like(forcing[0])
    result = adjoint_state + jnp.stack(
        [forcing[0], forcing[1], blank_field, blank_field, forcing[2]]
    )
    next_x, last_x = shifted(trajectory, trajectory, "gx", 3)
    next_y, last_y = shifted(trajectory, trajectory, "gy", 4)
    slope_x, slope_y = 0.5 * (next_x - last_x), 0.5 * (next_y - last_y)
    for section in (1, 0):
        result = adjoint_step(result, trajectory[section], slope_x[section], slope_y[section])
    return result


def solution(mesh):
    return jax.shard_map(
        local,
        mesh=mesh,
        in_specs=(
            P(None, None, "gx", "gy"),
            P(None, None, None, "gx", "gy"),
            P(("gx", "gy"), None, None),
            P(("gx", "gy"), None),
            P(("gx", "gy"), None),
            P(("gx", "gy"), None),
            P(("gx", "gy"), None),
        ),
        out_specs=P(None, None, "gx", "gy"),
        check_vma=False,
    )
```
